256 devices in a mesh: prow: 16 (over y, z_hi), pcol: 16 (over x, z_lo, core).
Axes of the slice: x: 4, y: 4, z: 8 (z_hi: 4, z_lo: 2; z = z_hi * 2 + z_lo), core: 2. Of those that a mesh axis runs over, the one named last changes fastest.
Arguments:
- covariance: float32 [96, 16, 64, 4096], P(None, 'prow', None, 'pcol'), may hold values from -32 to 6208, as said below
Outputs:
- factored: float32 [96, 16, 64, 4096], P(None, 'prow', None, 'pcol')
The draws below stay inside these ranges and needn't reach their ends.
Inputs may be any that keep to these rules, and one draw needn't show every extreme that they name: `covariance`: in the leading 2 * 64 columns every diagonal entry exceeds 2 * 64 times the largest magnitude of the other entries of those columns, so the leading block of order 2 * 64 is positive definite.
All inputs are finite; a program needn't handle non-finite values.
Results may differ from the reference program's by a relative error of at most 0.0003.
Values sent between devices are 32-bit elements; how exact they have to be, the bound alone decides.
No kernel may reach another device: no remote copies, remote signals or barrier semaphores. Data moves between devices by JAX's collectives and lax.ppermute only.
A program may use at most 128 MiB of HBM per device.

```python
import jax
import jax.numpy as jnp
from jax import lax

NB = 64
RBD = 96
ORDER = 98304
COLS = 4096
N_PROW = 16


def draw_covariance(key, part):
    key = jax.random.fold_in(key, 7)
    shape = (RBD, N_PROW, NB, COLS)
    first_key, second_key = jax.random.split(key, 2)
    row_ids = (lax.broadcasted_iota(jnp.int32, (RBD, N_PROW, NB, 1), 0) * N_PROW + lax.broadcasted_iota(jnp.int32, (RBD, N_PROW, NB, 1), 1)) * NB + lax.broadcasted_iota(jnp.int32, (RBD, N_PROW, NB, 1), 2)
    col_ids = lax.broadcasted_iota(jnp.int32, (1, 1, 1, COLS), 3)
    rough = jax.random.uniform(first_key, shape, minval=-1.0, maxval=1.0)
    level = jax.random.uniform(second_key, shape)
    in_panel = col_ids < 2 * NB
    off_value = jnp.where(in_panel, 32.0 * rough, rough)
    diag_value = jnp.where(in_panel, 32.0 * (2 * NB + 2 + NB * level), 10.0 + 4.0 * level)
    return jnp.where(row_ids == col_ids, diag_value, off_value).astype(jnp.float32)


def setup_inputs(seed: int = 0) -> dict:
    splits = jax.random.split(jax.random.key(seed), 2)
    return {
        "covariance": draw_covariance(jax.random.fold_in(splits[1], 71), 0),
    }


def reduce_panel(state, section):
    start_col = section * NB
    stop_col = start_col + NB
    corner = state[start_col:stop_col, start_col:stop_col]
    symmetric = jnp.tril(corner) + jnp.tril(corner, -1).T
    factor_low = jnp.linalg.cholesky(symmetric)
    inverse = jax.scipy.linalg.solve_triangular(factor_low, jnp.eye(NB, dtype=jnp.float32), lower=True)
    panel = jnp.dot(state[:, start_col:stop_col], inverse.T, precision=lax.Precision.HIGHEST)
    panel = panel.at[start_col:stop_col].set(factor_low)
    leading = panel[:COLS]
    col_ids = jnp.arange(COLS, dtype=jnp.int32)
    row_len = RBD * NB

    def update_rows(pieces):
        rows_state, rows_panel, first_row = pieces
        row_ids = first_row + jnp.arange(row_len, dtype=jnp.int32)
        product = jnp.dot(rows_panel, leading.T, precision=lax.Precision.HIGHEST)
        lower = row_ids[:, None] >= col_ids[None, :]
        update_mask = lower & (col_ids >= stop_col)[None, :]
        changed = jnp.where(update_mask, rows_state - product, rows_state)
        panel_cols = jnp.where(lower[:, start_col:stop_col], rows_panel, changed[:, start_col:stop_col])
        return changed.at[:, start_col:stop_col].set(panel_cols)
    blocks = lax.map(update_rows, (state.reshape(N_PROW, row_len, COLS), panel.reshape(N_PROW, row_len, NB), jnp.arange(N_PROW, dtype=jnp.int32) * row_len))
    return blocks.reshape(ORDER, COLS)

def reference(covariance):
    state = covariance.reshape(ORDER, COLS)
    for section in range(2):
        state = reduce_panel(state, section)
    return state.reshape(RBD, N_PROW, NB, COLS)
```

```python
import functools

import jax
import jax.numpy as jnp
from jax import lax
from jax.experimental import pallas as pl
from jax.experimental.pallas import tpu as pltpu
from jax.sharding import PartitionSpec as P

AXES = ("prow", "pcol")
NP, NQ = 16, 16
NB = 64
W2 = 2 * NB
PIECES = 8
F32 = jnp.float32
HI = lax.Precision.HIGHEST


def chip_move(chip, dx, dz):
    x, z = chip // 2, chip % 2
    return ((x + dx) % 4) * 2 + (z + dz) % 2


def over_pcol(value, pairs):
    flat = [(p * NQ + s, p * NQ + d) for p in range(NP) for s, d in pairs]
    return lax.ppermute(value, AXES, flat)


def over_prow(value, pairs):
    flat = [(s * NQ + q, d * NQ + q) for q in range(NQ) for s, d in pairs]
    return lax.ppermute(value, AXES, flat)


def factor_kernel(q_ref, corner_ref, lead_ref, m_ref, l_ref):
    raw = corner_ref[...]
    r = lax.broadcasted_iota(jnp.int32, (W2, W2), 0)
    c = lax.broadcasted_iota(jnp.int32, (W2, W2), 1)
    sym = jnp.where(r >= c, raw, jnp.where(r >= c, raw, 0.0).T)
    eye = jnp.where(r == c, 1.0, 0.0).astype(F32)
    full = jnp.concatenate([sym, eye], axis=1)
    tiles = [full[8 * t : 8 * t + 8] for t in range(W2 // 8)]
    sub = lax.broadcasted_iota(jnp.int32, (8, 1), 0)
    done = []
    for j in range(W2):
        t0, s0 = divmod(j, 8)
        row = tiles[t0][s0 : s0 + 1]
        row = row * lax.rsqrt(row[:, j : j + 1])
        done.append(row)
        inv = lax.rsqrt(tiles[t0][s0 : s0 + 1, j : j + 1])
        for t in range(t0, W2 // 8):
            col = tiles[t][:, j : j + 1] * inv
            if t == t0:
                col = jnp.where(sub > s0, col, 0.0)
            tiles[t] = tiles[t] - col * row
    rows = jnp.concatenate(done, axis=0)
    upper = jnp.where(r <= c, rows[:, :W2], 0.0)
    linv = jnp.where(r >= c, rows[:, W2:], 0.0)
    l_ref[...] = upper.T
    y = lax.dot_general(
        linv, lead_ref[...], (((1,), (1,)), ((), ())), precision=HI, preferred_element_type=F32
    )
    on_first = q_ref[0] == 0
    y = jnp.concatenate([jnp.where(on_first, -eye, y[:, :W2]), y[:, W2:]], axis=1)
    m_ref[...] = lax.dot_general(
        linv, y, (((0,), (0,)), ((), ())), precision=HI, preferred_element_type=F32
    )


def update_kernel(info, m_ref, l_ref, *refs):
    bufs, s_ref, o_ref, mhh, mlo = refs[:9], refs[9], refs[10], refs[11], refs[12]
    i = pl.program_id(0)
    block, core, p, q = info[i], info[8], info[9], info[10]

    @pl.when(i == 0)
    def _():
        m = m_ref[...]
        hi = m.astype(jnp.bfloat16)
        mhh[0:W2] = hi
        mhh[W2 : 2 * W2] = hi
        mlo[...] = (m - hi.astype(F32)).astype(jnp.bfloat16)

    rows, cols = s_ref.shape

    def run(buf):
        x = buf[...]
        hi = x.astype(jnp.bfloat16)
        lo = (x - hi.astype(F32)).astype(jnp.bfloat16)
        prod = jnp.dot(jnp.concatenate([hi, lo], axis=1), mhh[...], preferred_element_type=F32)
        prod += jnp.dot(hi, mlo[...], preferred_element_type=F32)
        old = s_ref[...]
        lane = lax.broadcasted_iota(jnp.int32, (1, cols), 1)
        replaced = (q == 0) & (lane < W2)
        o_ref[...] = jnp.where(replaced, 0.0, old) - prod

    for k in range(9):
        if k == 0:
            pick = i == 0
        elif k <= 2:
            pick = (i == 1) & (core == k - 1)
        else:
            pick = i == k - 1
        pl.when(pick)(functools.partial(run, bufs[k]))

    @pl.when(block == 0)
    def _():
        top = 4 * NB
        rr = lax.broadcasted_iota(jnp.int32, (top, cols), 0)
        cc = lax.broadcasted_iota(jnp.int32, (top, cols), 1) + q * cols
        rg = ((rr // NB) * NP + p) * NB + rr % NB
        o_ref[0:top] = jnp.where(rg >= cc, o_ref[0:top], s_ref[0:top])

    @pl.when((block == 0) & (q == 0) & (p < 2))
    def _():
        rr = lax.broadcasted_iota(jnp.int32, (NB, W2), 0) + p * NB
        cc = lax.broadcasted_iota(jnp.int32, (NB, W2), 1)
        part = l_ref[pl.ds(pl.multiple_of(p * NB, NB), NB), :]
        o_ref[0:NB, 0:W2] = jnp.where(rr >= cc, part, s_ref[0:NB, 0:W2])


def body(covariance):
    row_blocks, single, nb, cols = covariance.shape
    rows = row_blocks * nb
    local = covariance.reshape(rows, cols)
    p = lax.axis_index("prow")
    q = lax.axis_index("pcol")
    y, z = p // 4, p % 4
    chip, core = q // 2, q % 2
    part = rows // PIECES
    is_src = q == 0

    top = jnp.where(is_src, local[: 4 * NB, :W2], 0.0)
    have = [0]
    for bit in (1, 2, 4, 8):
        top = top + over_pcol(top, [(s, s + bit) for s in have])
        have = have + [s + bit for s in have]

    mine = jnp.where(is_src, local[:part, :W2], 0.0)
    for g in range(1, PIECES):
        mine = mine + over_pcol(local[g * part : (g + 1) * part, :W2], [(0, 2 * g)])
    both = mine + over_pcol(mine, [(2 * g, 2 * g + 1) for g in range(PIECES)])
    swap = [(s, s ^ 1) for s in range(NQ)]
    far = over_pcol(mine, [(2 * g, 2 * chip_move(g, 2, 1)) for g in range(PIECES)])
    far_s = over_pcol(far, swap)
    moves = [((1, 0), (-1, 0)), ((0, 1), (2, 0)), ((1, 1), (-1, 1))]
    bufs = [both, far, far_s]
    owners = [chip, (chip // 2 + 2) % 4 * 2 + 1 - chip % 2]
    for m0, m1 in moves:
        pairs = [(2 * g, 2 * chip_move(g, *m0)) for g in range(PIECES)]
        pairs += [(2 * g + 1, 2 * chip_move(g, *m1) + 1) for g in range(PIECES)]
        got = over_pcol(both, pairs)
        bufs += [got, over_pcol(got, swap)]
        own = [((chip // 2 - m[0]) % 4) * 2 + (chip + m[1]) % 2 for m in (m0, m1)]
        owners += [jnp.where(core == 0, own[0], own[1]), jnp.where(core == 0, own[1], own[0])]

    root = q % 4
    lead = lax.dynamic_slice_in_dim(top, (q // 4) * NB, NB, 0)
    pack = jnp.stack([lead, top[:NB]])
    got = over_prow(pack, [(s, s ^ 4) for s in range(NP)])
    use = jnp.stack([y == root ^ 1, y == 1])
    pack = jnp.where(use[:, None, None], got, pack)
    got = over_prow(pack, [(s, s ^ 8) for s in range(NP)])
    use = jnp.stack([y // 2 != root // 2, y >= 2])
    pack = jnp.where(use[:, None, None], got, pack)
    got = over_prow(pack, [(s, s ^ 1) for s in range(NP)])
    odd = z % 2 == 1
    pack = jnp.where(odd, jnp.stack([got, pack]), jnp.stack([pack, got]))
    got = over_prow(pack, [(s, s ^ 2) for s in range(NP)])
    high = z >= 2
    lead = jnp.where(
        high, jnp.stack([got[:, 0], pack[:, 0]]), jnp.stack([pack[:, 0], got[:, 0]])
    ).reshape(4 * NB, W2)
    corner = jnp.where(high, got[:, 1], pack[:, 1]).reshape(W2, W2)

    smem = pl.BlockSpec(memory_space=pltpu.SMEM)
    vmem = pl.BlockSpec(memory_space=pltpu.VMEM)
    weights, low = pl.pallas_call(
        factor_kernel,
        out_shape=(jax.ShapeDtypeStruct((W2, cols), F32), jax.ShapeDtypeStruct((W2, W2), F32)),
        in_specs=[smem, vmem, vmem],
        out_specs=(vmem, vmem),
        name="factor",
    )(q.reshape(1).astype(jnp.int32), corner, lead)

    info = jnp.stack([o.astype(jnp.int32) for o in owners + [core, p, q]])
    whole = lambda shape: pl.BlockSpec(shape, lambda i, s: (0, 0))
    tile = pl.BlockSpec((part, cols), lambda i, s: (s[i], 0))
    out = pl.pallas_call(
        update_kernel,
        out_shape=jax.ShapeDtypeStruct((rows, cols), F32),
        grid_spec=pltpu.PrefetchScalarGridSpec(
            num_scalar_prefetch=1,
            grid=(PIECES,),
            in_specs=[whole((W2, cols)), whole((W2, W2))] + [whole((part, W2))] * 9 + [tile],
            out_specs=tile,
            scratch_shapes=[
                pltpu.VMEM((2 * W2, cols), jnp.bfloat16),
                pltpu.VMEM((W2, cols), jnp.bfloat16),
            ],
        ),
        compiler_params=pltpu.CompilerParams(vmem_limit_bytes=40 * 1024 * 1024),
        name="update",
    )(info, weights, low, *bufs, local)
    return out.reshape(row_blocks, single, nb, cols)


def solution(mesh):
    spec = P(None, "prow", None, "pcol")
    return jax.shard_map(body, mesh=mesh, in_specs=(spec,), out_specs=spec, check_vma=False)
```

```python
import functools

import jax
import jax.numpy as jnp
from jax import lax
from jax.experimental import pallas as pl
from jax.experimental.pallas import tpu as pltpu
from jax.sharding import PartitionSpec as P

AXES = ("prow", "pcol")
NP, NQ = 16, 16
NB = 64
W2 = 2 * NB
PIECES = 8
F32 = jnp.float32
BF16 = jnp.bfloat16
HI = lax.Precision.HIGHEST


def chip_move(chip, dx, dz):
    x, z = chip // 2, chip % 2
    return ((x + dx) % 4) * 2 + (z + dz) % 2


def over_pcol(value, pairs):
    flat = [(p * NQ + s, p * NQ + d) for p in range(NP) for s, d in pairs]
    return lax.ppermute(value, AXES, flat)


def over_prow(value, pairs):
    flat = [(s * NQ + q, d * NQ + q) for q in range(NQ) for s, d in pairs]
    return lax.ppermute(value, AXES, flat)


def factor(raw):
    r = lax.broadcasted_iota(jnp.int32, (W2, W2), 0)
    c = lax.broadcasted_iota(jnp.int32, (W2, W2), 1)
    low = jnp.where(r >= c, raw, 0.0)
    sym = jnp.where(r >= c, low, low.T)
    eye = jnp.where(r == c, 1.0, 0.0).astype(F32)
    nt = W2 // 8
    left = [sym[8 * t : 8 * t + 8] for t in range(nt)]
    right = [eye[8 * t : 8 * t + 8] for t in range(nt)]
    sub = lax.broadcasted_iota(jnp.int32, (8, W2), 0)
    up, inv_rows = [], []
    for k in range(nt):
        cols = {}
        for t in range(k, nt):
            for j in range(8):
                a = left[t][:, 8 * k + j : 8 * k + j + 1]
                cols[t, j] = jnp.broadcast_to(a, (8, W2))
        for s in range(8):
            inv = lax.rsqrt(cols[k, s][s : s + 1])
            lrow = left[k][s : s + 1] * inv
            rrow = right[k][s : s + 1] * inv
            up.append(lrow)
            inv_rows.append(rrow)
            pivots = {j: cols[k, j][s : s + 1] * inv for j in range(s + 1, 8)}
            for t in range(k, nt):
                f = cols[t, s] * inv
                if t == k:
                    f = jnp.where(sub > s, f, 0.0)
                for j in range(s + 1, 8):
                    cols[t, j] = cols[t, j] - f * pivots[j]
                left[t] = left[t] - f * lrow
                right[t] = right[t] - f * rrow
    upper = jnp.where(r <= c, jnp.concatenate(up, axis=0), 0.0)
    linv = jnp.where(r >= c, jnp.concatenate(inv_rows, axis=0), 0.0)
    return upper.T, linv, eye


def pack_kernel(chips, local, *refs):
    outs, sem = refs[:-1], refs[-1]
    part = outs[0].shape[0] - W2
    copies = []
    for k, g in enumerate(chips):
        for j, (src, dst, n) in enumerate(
            ((g * part, 0, part), (0, part, NB), (g // 2 * NB, part + NB, NB))
        ):
            copies.append(
                pltpu.make_async_copy(
                    local.at[pl.ds(src, n), pl.ds(0, W2)], outs[k].at[pl.ds(dst, n)], sem.at[k, j]
                )
            )
    for copy in copies:
        copy.start()
    for copy in copies:
        copy.wait()


def finish_kernel(
    info, corner_ref, lead_ref, *refs
):
    bufs, state, out = refs[:9], refs[9], refs[10]
    x_v, s_v, o_v, mhh, mlo, low_v, x_sem, s_sem, o_sem = refs[11:]
    rows, cols = s_v.shape[1:]
    core, p, q = info[8], info[9], info[10]

    def place(k):
        return pl.ds(pl.multiple_of(info[k] * rows, rows), rows)

    def load_s(k):
        return pltpu.make_async_copy(state.at[place(k)], s_v.at[k], s_sem.at[k])

    def load_x(k, ref):
        return pltpu.make_async_copy(ref, x_v.at[k], x_sem.at[k])

    def store(k):
        return pltpu.make_async_copy(o_v.at[k], out.at[place(k)], o_sem.at[k])

    for k in range(PIECES):
        load_s(k).start()
    load_x(0, bufs[0]).start()

    @pl.when(core == 0)
    def _():
        load_x(1, bufs[1]).start()

    @pl.when(core == 1)
    def _():
        load_x(1, bufs[2]).start()

    for k in range(2, PIECES):
        load_x(k, bufs[k + 1]).start()

    low, linv, eye = factor(corner_ref[...])
    low_v[...] = low
    y = lax.dot_general(
        linv, lead_ref[...], (((1,), (1,)), ((), ())), precision=HI, preferred_element_type=F32
    )
    y = jnp.concatenate([jnp.where(q == 0, -eye, y[:, :W2]), y[:, W2:]], axis=1)
    m = lax.dot_general(
        linv, y, (((0,), (0,)), ((), ())), precision=HI, preferred_element_type=F32
    )
    hi = m.astype(BF16)
    mhh[0:W2] = hi
    mhh[W2 : 2 * W2] = hi
    mlo[...] = (m - hi.astype(F32)).astype(BF16)

    def piece(k, carry):
        load_s(k).wait()
        load_x(k, bufs[0]).wait()
        x = x_v[k]
        xh = x.astype(BF16)
        xl = (x - xh.astype(F32)).astype(BF16)
        prod = jnp.dot(jnp.concatenate([xh, xl], axis=1), mhh[...], preferred_element_type=F32)
        prod += jnp.dot(xh, mlo[...], preferred_element_type=F32)
        lane = lax.broadcasted_iota(jnp.int32, (1, cols), 1)
        replaced = (q == 0) & (lane < W2)
        o_v[k] = jnp.where(replaced, 0.0, s_v[k]) - prod

        @pl.when(info[k] == 0)
        def _():
            top = 4 * NB
            rr = lax.broadcasted_iota(jnp.int32, (top, cols), 0)
            cc = lax.broadcasted_iota(jnp.int32, (top, cols), 1) + q * cols
            rg = ((rr // NB) * NP + p) * NB + rr % NB
            o_v[k, 0:top] = jnp.where(rg >= cc, o_v[k, 0:top], s_v[k, 0:top])

        @pl.when((info[k] == 0) & (q == 0) & (p < 2))
        def _():
            rr = lax.broadcasted_iota(jnp.int32, (NB, W2), 0) + p * NB
            cc = lax.broadcasted_iota(jnp.int32, (NB, W2), 1)
            part = low_v[pl.ds(pl.multiple_of(jnp.minimum(p, 1) * NB, NB), NB), :]
            o_v[k, 0:NB, 0:W2] = jnp.where(rr >= cc, part, s_v[k, 0:NB, 0:W2])

        store(k).start()
        return carry

    lax.fori_loop(0, PIECES, piece, 0)
    for k in range(PIECES):
        store(k).wait()


def body(covariance):
    row_blocks, single, nb, cols = covariance.shape
    rows = row_blocks * nb
    local = covariance.reshape(rows, cols)
    p = lax.axis_index("prow")
    q = lax.axis_index("pcol")
    y, z = p // 4, p % 4
    chip, core = q // 2, q % 2
    part = rows // PIECES
    is_src = q == 0
    smem = pl.BlockSpec(memory_space=pltpu.SMEM)
    vmem = pl.BlockSpec(memory_space=pltpu.VMEM)
    hbm = pl.BlockSpec(memory_space=pl.ANY)

    messages = {}
    for chips in ((3, 7, 5), (4, 6, 1, 2, 0)):
        got = pl.pallas_call(
            functools.partial(pack_kernel, chips),
            out_shape=[jax.ShapeDtypeStruct((part + W2, W2), F32)] * len(chips),
            in_specs=[hbm],
            out_specs=[vmem] * len(chips),
            scratch_shapes=[pltpu.SemaphoreType.DMA((len(chips), 3))],
            name="pack",
        )(local)
        messages.update(zip(chips, got))
    relay = over_pcol(messages[3], [(0, 5)]) + over_pcol(messages[7], [(0, 13)])
    mine = jnp.where(is_src, messages[0], 0.0)
    for g in (5, 4, 6, 1, 2):
        mine = mine + over_pcol(messages[g], [(0, 2 * g)])
    mine = mine + over_pcol(relay, [(5, 6), (13, 14)])
    lend = [(2 * g, 2 * g + 1) for g in range(PIECES)]
    mine = mine + over_pcol(mine, lend)
    both = mine[:part]
    pack = mine[part:].reshape(2, NB, W2)

    root = q % 4
    got = over_prow(pack, [(s, s ^ 4) for s in range(NP)])
    pack = jnp.stack([jnp.where(y == 1, got[0], pack[0]), jnp.where(y == root ^ 1, got[1], pack[1])])
    got = over_prow(pack, [(s, s ^ 12) for s in range(NP)])
    pack = jnp.stack(
        [jnp.where(y >= 2, got[0], pack[0]), jnp.where(y // 2 != root // 2, got[1], pack[1])]
    )
    got = over_prow(pack, [(s, s ^ 1) for s in range(NP)])
    odd = z % 2 == 1
    pack = jnp.where(odd, jnp.stack([got, pack], 1), jnp.stack([pack, got], 1))
    got = over_prow(pack, [(s, s ^ 3) for s in range(NP)])
    high = z >= 2
    corner = jnp.where(high, got[0], pack[0]).reshape(W2, W2)
    lead = jnp.concatenate(
        [jnp.where(high, got, pack)[1], jnp.where(high, pack, got)[1]]
    ).reshape(4 * NB, W2)

    swap = [(s, s ^ 1) for s in range(NQ)]

    def send(value, m0, m1):
        pairs = [(2 * g, 2 * chip_move(g, *m0)) for g in range(PIECES)]
        if m1 is not None:
            pairs += [(2 * g + 1, 2 * chip_move(g, *m1) + 1) for g in range(PIECES)]
        return over_pcol(value, pairs)

    def owner(m0, m1):
        own = [((chip // 2 - m[0]) % 4) * 2 + (chip + m[1]) % 2 for m in (m0, m1)]
        return [jnp.where(core == 0, own[0], own[1]), jnp.where(core == 0, own[1], own[0])]

    side = send(both, (1, 0), (-1, 0))
    later = both
    cross = send(later, (1, 1), (-1, 1))
    over = send(later, (0, 1), None)
    again = send(jnp.where(core == 0, side, cross), (1, 0), (-1, 0))
    bufs = [both, over, over_pcol(over, lend)]
    owners = [chip, chip // 2 * 2 + 1 - chip % 2]
    for got, moves in (
        (side, ((1, 0), (-1, 0))),
        (cross, ((1, 1), (-1, 1))),
        (again, ((2, 0), (-2, 1))),
    ):
        bufs += [got, over_pcol(got, swap)]
        owners += owner(*moves)

    info = jnp.stack([o.astype(jnp.int32) for o in owners + [core, p, q]])
    out = pl.pallas_call(
        finish_kernel,
        out_shape=jax.ShapeDtypeStruct((rows, cols), F32),
        in_specs=[smem, vmem, vmem] + [hbm] * 10,
        out_specs=hbm,
        scratch_shapes=[
            pltpu.VMEM((PIECES, part, W2), F32),
            pltpu.VMEM((PIECES, part, cols), F32),
            pltpu.VMEM((PIECES, part, cols), F32),
            pltpu.VMEM((2 * W2, cols), BF16),
            pltpu.VMEM((W2, cols), BF16),
            pltpu.VMEM((W2, W2), F32),
            pltpu.SemaphoreType.DMA((PIECES,)),
            pltpu.SemaphoreType.DMA((PIECES,)),
            pltpu.SemaphoreType.DMA((PIECES,)),
        ],
        compiler_params=pltpu.CompilerParams(vmem_limit_bytes=52 * 1024 * 1024),
        name="finish",
    )(info, corner, lead, *bufs, local)
    return out.reshape(row_blocks, single, nb, cols)


def solution(mesh):
    spec = P(None, "prow", None, "pcol")
    return jax.shard_map(body, mesh=mesh, in_specs=(spec,), out_specs=spec, check_vma=False)
```

```python
import functools

import jax
import jax.numpy as jnp
from jax import lax
from jax.experimental import pallas as pl
from jax.experimental.pallas import tpu as pltpu
from jax.sharding import PartitionSpec as P

AXES = ("prow", "pcol")
NP, NQ = 16, 16
NB = 64
W2 = 2 * NB
PIECES = 8
F32 = jnp.float32
BF16 = jnp.bfloat16
HI = lax.Precision.HIGHEST


def chip_move(chip, dx, dz):
    x, z = chip // 2, chip % 2
    return ((x + dx) % 4) * 2 + (z + dz) % 2


def over_pcol(value, pairs):
    flat = [(p * NQ + s, p * NQ + d) for p in range(NP) for s, d in pairs]
    return lax.ppermute(value, AXES, flat)


def over_prow(value, pairs):
    flat = [(s * NQ + q, d * NQ + q) for q in range(NQ) for s, d in pairs]
    return lax.ppermute(value, AXES, flat)


def factor(raw):
    r = lax.broadcasted_iota(jnp.int32, (W2, W2), 0)
    c = lax.broadcasted_iota(jnp.int32, (W2, W2), 1)
    low = jnp.where(r >= c, raw, 0.0)
    sym = jnp.where(r >= c, low, low.T)
    eye = jnp.where(r == c, 1.0, 0.0).astype(F32)
    nt = W2 // 8
    left = [sym[8 * t : 8 * t + 8] for t in range(nt)]
    right = [eye[8 * t : 8 * t + 8] for t in range(nt)]
    sub = lax.broadcasted_iota(jnp.int32, (8, W2), 0)
    up, inv_rows = [], []
    for k in range(nt):
        cols = {}
        for t in range(k, nt):
            for j in range(8):
                a = left[t][:, 8 * k + j : 8 * k + j + 1]
                cols[t, j] = jnp.broadcast_to(a, (8, W2))
        for s in range(0, 8, 2):
            d0 = cols[k, s][s : s + 1]
            e = cols[k, s][s + 1 : s + 2]
            d1 = cols[k, s + 1][s + 1 : s + 2]
            det = d0 * d1 - e * e
            inv0 = lax.rsqrt(d0)
            inv1 = lax.rsqrt(det) * (d0 * inv0)
            lo0, ro0 = left[k][s : s + 1] * inv0, right[k][s : s + 1] * inv0
            f10 = e * inv0
            lo1 = (left[k][s + 1 : s + 2] - f10 * lo0) * inv1
            ro1 = (right[k][s + 1 : s + 2] - f10 * ro0) * inv1
            up += [lo0, lo1]
            inv_rows += [ro0, ro1]
            piv = {}
            for j in range(s + 2, 8):
                p0 = cols[k, j][s : s + 1] * inv0
                piv[j] = (p0, (cols[k, j][s + 1 : s + 2] - f10 * p0) * inv1)
            for t in range(k, nt):
                f0 = cols[t, s] * inv0
                f1 = (cols[t, s + 1] - f0 * f10) * inv1
                if t == k:
                    f0 = jnp.where(sub > s + 1, f0, 0.0)
                    f1 = jnp.where(sub > s + 1, f1, 0.0)
                for j in range(s + 2, 8):
                    cols[t, j] = cols[t, j] - f0 * piv[j][0] - f1 * piv[j][1]
                left[t] = left[t] - f0 * lo0 - f1 * lo1
                right[t] = right[t] - f0 * ro0 - f1 * ro1
    upper = jnp.where(r <= c, jnp.concatenate(up, axis=0), 0.0)
    linv = jnp.where(r >= c, jnp.concatenate(inv_rows, axis=0), 0.0)
    return upper.T, linv, eye


def pack_kernel(chips, q_ref, local, *refs):
    outs, (held, in_sem, out_sem) = refs[:-3], refs[-3:]
    part = outs[0].shape[0] - W2

    @pl.when(q_ref[0] == 0)
    def _():
        ins, copies = [], []
        for k, g in enumerate(chips):
            ins.append([])
            for j, (src, dst, n) in enumerate(
                ((g * part, 0, part), (0, part, NB), (g // 2 * NB, part + NB, NB))
            ):
                ins[k].append(
                    pltpu.make_async_copy(
                        local.at[pl.ds(src, n), pl.ds(0, W2)],
                        held.at[k, pl.ds(dst, n)],
                        in_sem.at[k, j],
                    )
                )
                ins[k][j].start()
        for k in range(len(chips)):
            for copy in ins[k]:
                copy.wait()
            copies.append(pltpu.make_async_copy(held.at[k], outs[k], out_sem.at[k]))
            copies[k].start()
        for copy in copies:
            copy.wait()


def finish_kernel(
    info, corner_ref, lead_ref, *refs
):
    bufs, state, out = refs[:9], refs[9], refs[10]
    x_v, s_v, o_v, w_v, low_v, x_sem, s_sem, o_sem = refs[11:]
    rows, cols = s_v.shape[1:]
    core, p, q = info[8], info[9], info[10]

    def place(k):
        return pl.ds(pl.multiple_of(info[k] * rows, rows), rows)

    def load_s(k):
        return pltpu.make_async_copy(state.at[place(k)], s_v.at[k], s_sem.at[k])

    def load_x(k, ref):
        return pltpu.make_async_copy(ref, x_v.at[k], x_sem.at[k])

    def store(k):
        return pltpu.make_async_copy(o_v.at[k], out.at[place(k)], o_sem.at[k])

    for k in range(PIECES):
        load_s(k).start()
    load_x(0, bufs[0]).start()

    @pl.when(core == 0)
    def _():
        load_x(1, bufs[1]).start()

    @pl.when(core == 1)
    def _():
        load_x(1, bufs[2]).start()

    for k in range(2, PIECES):
        load_x(k, bufs[k + 1]).start()

    low, linv, eye = factor(corner_ref[...])
    low_v[...] = low
    y = lax.dot_general(
        linv, lead_ref[...], (((1,), (1,)), ((), ())), precision=HI, preferred_element_type=F32
    )
    y = jnp.concatenate([jnp.where(q == 0, -eye, y[:, :W2]), y[:, W2:]], axis=1)
    m = lax.dot_general(
        linv, y, (((0,), (0,)), ((), ())), precision=HI, preferred_element_type=F32
    )
    hi = m.astype(BF16)
    w_v[0:W2] = hi
    w_v[W2 : 2 * W2] = hi
    w_v[2 * W2 :] = (m - hi.astype(F32)).astype(BF16)

    def piece(k, carry):
        load_s(k).wait()
        load_x(k, bufs[0]).wait()
        x = x_v[k]
        xh = x.astype(BF16)
        xl = (x - xh.astype(F32)).astype(BF16)
        prod = jnp.dot(jnp.concatenate([xh, xl, xh], axis=1), w_v[...], preferred_element_type=F32)
        lane = lax.broadcasted_iota(jnp.int32, (1, cols), 1)
        replaced = (q == 0) & (lane < W2)
        o_v[k] = jnp.where(replaced, 0.0, s_v[k]) - prod

        @pl.when(info[k] == 0)
        def _():
            top = 4 * NB
            rr = lax.broadcasted_iota(jnp.int32, (top, cols), 0)
            cc = lax.broadcasted_iota(jnp.int32, (top, cols), 1) + q * cols
            rg = ((rr // NB) * NP + p) * NB + rr % NB
            o_v[k, 0:top] = jnp.where(rg >= cc, o_v[k, 0:top], s_v[k, 0:top])

        @pl.when((info[k] == 0) & (q == 0) & (p < 2))
        def _():
            rr = lax.broadcasted_iota(jnp.int32, (NB, W2), 0) + p * NB
            cc = lax.broadcasted_iota(jnp.int32, (NB, W2), 1)
            part = low_v[pl.ds(pl.multiple_of(jnp.minimum(p, 1) * NB, NB), NB), :]
            o_v[k, 0:NB, 0:W2] = jnp.where(rr >= cc, part, s_v[k, 0:NB, 0:W2])

        store(k).start()
        return carry

    lax.fori_loop(0, PIECES, piece, 0)
    for k in range(PIECES):
        store(k).wait()


def body(covariance):
    row_blocks, single, nb, cols = covariance.shape
    rows = row_blocks * nb
    local = covariance.reshape(rows, cols)
    p = lax.axis_index("prow")
    q = lax.axis_index("pcol")
    y, z = p // 4, p % 4
    chip, core = q // 2, q % 2
    part = rows // PIECES
    is_src = q == 0
    smem = pl.BlockSpec(memory_space=pltpu.SMEM)
    vmem = pl.BlockSpec(memory_space=pltpu.VMEM)
    hbm = pl.BlockSpec(memory_space=pl.ANY)

    messages = {}
    for chips in ((3, 7, 2, 4, 5, 1, 6, 0),):
        got = pl.pallas_call(
            functools.partial(pack_kernel, chips),
            out_shape=[jax.ShapeDtypeStruct((part + W2, W2), F32)] * len(chips),
            in_specs=[smem, hbm],
            out_specs=[hbm] * len(chips),
            scratch_shapes=[
                pltpu.VMEM((len(chips), part + W2, W2), F32),
                pltpu.SemaphoreType.DMA((len(chips), 3)),
                pltpu.SemaphoreType.DMA((len(chips),)),
            ],
            name="pack",
        )(q.reshape(1).astype(jnp.int32), local)
        messages.update(zip(chips, got))
    relay = over_pcol(messages[3], [(0, 5)]) + over_pcol(messages[7], [(0, 13)])
    mine = jnp.where(is_src, messages[0], 0.0)
    for g in (2, 4, 5, 1, 6):
        mine = mine + over_pcol(messages[g], [(0, 2 * g)])
    mine = mine + over_pcol(relay, [(5, 6), (13, 14)])
    lend = [(2 * g, 2 * g + 1) for g in range(PIECES)]
    mine = mine + over_pcol(mine, lend)
    both = mine[:part]
    pack = mine[part:].reshape(2, NB, W2)

    root = q % 4
    got = over_prow(pack, [(s, s ^ 4) for s in range(NP)])
    pack = jnp.stack([jnp.where(y == 1, got[0], pack[0]), jnp.where(y == root ^ 1, got[1], pack[1])])
    got = over_prow(pack, [(s, s ^ 12) for s in range(NP)])
    pack = jnp.stack(
        [jnp.where(y >= 2, got[0], pack[0]), jnp.where(y // 2 != root // 2, got[1], pack[1])]
    )
    got = over_prow(pack, [(s, s ^ 1) for s in range(NP)])
    odd = z % 2 == 1
    pack = jnp.where(odd, jnp.stack([got, pack], 1), jnp.stack([pack, got], 1))
    got = over_prow(pack, [(s, s ^ 3) for s in range(NP)])
    high = z >= 2
    corner = jnp.where(high, got[0], pack[0]).reshape(W2, W2)
    lead = jnp.concatenate(
        [jnp.where(high, got, pack)[1], jnp.where(high, pack, got)[1]]
    ).reshape(4 * NB, W2)

    swap = [(s, s ^ 1) for s in range(NQ)]

    def send(value, m0, m1):
        pairs = [(2 * g, 2 * chip_move(g, *m0)) for g in range(PIECES)]
        if m1 is not None:
            pairs += [(2 * g + 1, 2 * chip_move(g, *m1) + 1) for g in range(PIECES)]
        return over_pcol(value, pairs)

    def owner(m0, m1):
        own = [((chip // 2 - m[0]) % 4) * 2 + (chip + m[1]) % 2 for m in (m0, m1)]
        return [jnp.where(core == 0, own[0], own[1]), jnp.where(core == 0, own[1], own[0])]

    side = send(both, (1, 0), (-1, 0))
    later = both
    cross = send(later, (1, 1), (-1, 1))
    over = send(later, (0, 1), None)
    again = send(jnp.where(core == 0, side, cross), (1, 0), (-1, 0))
    bufs = [both, over, over_pcol(over, lend)]
    owners = [chip, chip // 2 * 2 + 1 - chip % 2]
    for got, moves in (
        (side, ((1, 0), (-1, 0))),
        (cross, ((1, 1), (-1, 1))),
        (again, ((2, 0), (-2, 1))),
    ):
        bufs += [got, over_pcol(got, swap)]
        owners += owner(*moves)

    info = jnp.stack([o.astype(jnp.int32) for o in owners + [core, p, q]])
    out = pl.pallas_call(
        finish_kernel,
        out_shape=jax.ShapeDtypeStruct((rows, cols), F32),
        in_specs=[smem, vmem, vmem] + [hbm] * 10,
        out_specs=hbm,
        scratch_shapes=[
            pltpu.VMEM((PIECES, part, W2), F32),
            pltpu.VMEM((PIECES, part, cols), F32),
            pltpu.VMEM((PIECES, part, cols), F32),
            pltpu.VMEM((3 * W2, cols), BF16),
            pltpu.VMEM((W2, W2), F32),
            pltpu.SemaphoreType.DMA((PIECES,)),
            pltpu.SemaphoreType.DMA((PIECES,)),
            pltpu.SemaphoreType.DMA((PIECES,)),
        ],
        compiler_params=pltpu.CompilerParams(vmem_limit_bytes=52 * 1024 * 1024),
        name="finish",
    )(info, corner, lead, *bufs, local)
    return out.reshape(row_blocks, single, nb, cols)


def solution(mesh):
    spec = P(None, "prow", None, "pcol")
    return jax.shard_map(body, mesh=mesh, in_specs=(spec,), out_specs=spec, check_vma=False)
```

```python
import functools

import jax
import jax.numpy as jnp
from jax import lax
from jax.experimental import pallas as pl
from jax.experimental.pallas import tpu as pltpu
from jax.sharding import PartitionSpec as P

AXES = ("prow", "pcol")
NP, NQ = 16, 16
NB = 64
W2 = 2 * NB
PIECES = 8
F32 = jnp.float32
BF16 = jnp.bfloat16
HI = lax.Precision.HIGHEST


def chip_move(chip, dx, dz):
    x, z = chip // 2, chip % 2
    return ((x + dx) % 4) * 2 + (z + dz) % 2


def over_pcol(value, pairs):
    flat = [(p * NQ + s, p * NQ + d) for p in range(NP) for s, d in pairs]
    return lax.ppermute(value, AXES, flat)


def over_prow(value, pairs):
    flat = [(s * NQ + q, d * NQ + q) for q in range(NQ) for s, d in pairs]
    return lax.ppermute(value, AXES, flat)


def factor(raw):
    r = lax.broadcasted_iota(jnp.int32, (W2, W2), 0)
    c = lax.broadcasted_iota(jnp.int32, (W2, W2), 1)
    low = jnp.where(r >= c, raw, 0.0)
    sym = jnp.where(r >= c, low, low.T)
    eye = jnp.where(r == c, 1.0, 0.0).astype(F32)
    nt = W2 // 8
    left = [sym[8 * t : 8 * t + 8] for t in range(nt)]
    right = [eye[8 * t : 8 * t + 8] for t in range(nt)]
    sub = lax.broadcasted_iota(jnp.int32, (8, W2), 0)
    up, inv_rows = [], []
    for k in range(nt):
        cols = {}
        for t in range(k, nt):
            for j in range(8):
                a = left[t][:, 8 * k + j : 8 * k + j + 1]
                cols[t, j] = jnp.broadcast_to(a, (8, W2))
        for s in range(0, 8, 2):
            d0 = cols[k, s][s : s + 1]
            e = cols[k, s][s + 1 : s + 2]
            d1 = cols[k, s + 1][s + 1 : s + 2]
            det = d0 * d1 - e * e
            inv0 = lax.rsqrt(d0)
            inv1 = lax.rsqrt(det) * (d0 * inv0)
            lo0, ro0 = left[k][s : s + 1] * inv0, right[k][s : s + 1] * inv0
            f10 = e * inv0
            lo1 = (left[k][s + 1 : s + 2] - f10 * lo0) * inv1
            ro1 = (right[k][s + 1 : s + 2] - f10 * ro0) * inv1
            up += [lo0, lo1]
            inv_rows += [ro0, ro1]
            piv = {}
            for j in range(s + 2, 8):
                p0 = cols[k, j][s : s + 1] * inv0
                piv[j] = (p0, (cols[k, j][s + 1 : s + 2] - f10 * p0) * inv1)
            for t in range(k, nt):
                f0 = cols[t, s] * inv0
                f1 = (cols[t, s + 1] - f0 * f10) * inv1
                if t == k:
                    f0 = jnp.where(sub > s + 1, f0, 0.0)
                    f1 = jnp.where(sub > s + 1, f1, 0.0)
                for j in range(s + 2, 8):
                    cols[t, j] = cols[t, j] - f0 * piv[j][0] - f1 * piv[j][1]
                left[t] = left[t] - f0 * lo0 - f1 * lo1
                right[t] = right[t] - f0 * ro0 - f1 * ro1
    upper = jnp.where(r <= c, jnp.concatenate(up, axis=0), 0.0)
    linv = jnp.where(r >= c, jnp.concatenate(inv_rows, axis=0), 0.0)
    return upper.T, linv, eye


def pack_kernel(chips, q_ref, local, *refs):
    outs, (held, in_sem, out_sem) = refs[:-3], refs[-3:]
    part = outs[0].shape[0] - W2

    @pl.when(q_ref[0] == 0)
    def _():
        ins, copies = [], []
        for k, g in enumerate(chips):
            ins.append([])
            for j, (src, dst, n) in enumerate(
                ((g * part, 0, part), (0, part, NB), (g // 2 * NB, part + NB, NB))
            ):
                ins[k].append(
                    pltpu.make_async_copy(
                        local.at[pl.ds(src, n), pl.ds(0, W2)],
                        held.at[k, pl.ds(dst, n)],
                        in_sem.at[k, j],
                    )
                )
                ins[k][j].start()
        for k in range(len(chips)):
            for copy in ins[k]:
                copy.wait()
            copies.append(pltpu.make_async_copy(held.at[k], outs[k], out_sem.at[k]))
            copies[k].start()
        for copy in copies:
            copy.wait()


def finish_kernel(
    info, corner_ref, lead_ref, *refs
):
    bufs, state, out = refs[:9], refs[9], refs[10]
    x_v, s_v, o_v, w_v, low_v, x_sem, s_sem, o_sem = refs[11:]
    rows, cols = s_v.shape[1:]
    core, p, q = info[8], info[9], info[10]

    def place(k):
        return pl.ds(pl.multiple_of(info[k] * rows, rows), rows)

    def load_s(k):
        return pltpu.make_async_copy(state.at[place(k)], s_v.at[k], s_sem.at[k])

    def load_x(k, ref):
        return pltpu.make_async_copy(ref, x_v.at[k], x_sem.at[k])

    def store(k):
        return pltpu.make_async_copy(o_v.at[k], out.at[place(k)], o_sem.at[k])

    for k in range(PIECES):
        load_s(k).start()
    load_x(0, bufs[0]).start()

    @pl.when(core == 0)
    def _():
        load_x(1, bufs[1]).start()

    @pl.when(core == 1)
    def _():
        load_x(1, bufs[2]).start()

    for k in range(2, PIECES):
        load_x(k, bufs[k + 1]).start()

    low, linv, eye = factor(corner_ref[...])
    low_v[...] = low
    y = lax.dot_general(
        linv, lead_ref[...], (((1,), (1,)), ((), ())), precision=HI, preferred_element_type=F32
    )
    y = jnp.concatenate([jnp.where(q == 0, -eye, y[:, :W2]), y[:, W2:]], axis=1)
    m = lax.dot_general(
        linv, y, (((0,), (0,)), ((), ())), precision=HI, preferred_element_type=F32
    )
    hi = m.astype(BF16)
    w_v[0:W2] = hi
    w_v[W2 : 2 * W2] = hi
    w_v[2 * W2 :] = (m - hi.astype(F32)).astype(BF16)

    def piece(k, carry):
        load_s(k).wait()
        load_x(k, bufs[0]).wait()
        x = x_v[k]
        xh = x.astype(BF16)
        xl = (x - xh.astype(F32)).astype(BF16)
        prod = jnp.dot(jnp.concatenate([xh, xl, xh], axis=1), w_v[...], preferred_element_type=F32)
        lane = lax.broadcasted_iota(jnp.int32, (1, cols), 1)
        replaced = (q == 0) & (lane < W2)
        o_v[k] = jnp.where(replaced, 0.0, s_v[k]) - prod

        @pl.when(info[k] == 0)
        def _():
            top = 4 * NB
            rr = lax.broadcasted_iota(jnp.int32, (top, cols), 0)
            cc = lax.broadcasted_iota(jnp.int32, (top, cols), 1) + q * cols
            rg = ((rr // NB) * NP + p) * NB + rr % NB
            o_v[k, 0:top] = jnp.where(rg >= cc, o_v[k, 0:top], s_v[k, 0:top])

        @pl.when((info[k] == 0) & (q == 0) & (p < 2))
        def _():
            rr = lax.broadcasted_iota(jnp.int32, (NB, W2), 0) + p * NB
            cc = lax.broadcasted_iota(jnp.int32, (NB, W2), 1)
            part = low_v[pl.ds(pl.multiple_of(jnp.minimum(p, 1) * NB, NB), NB), :]
            o_v[k, 0:NB, 0:W2] = jnp.where(rr >= cc, part, s_v[k, 0:NB, 0:W2])

        store(k).start()
        return carry

    lax.fori_loop(0, PIECES, piece, 0)
    for k in range(PIECES):
        store(k).wait()


def body(covariance):
    row_blocks, single, nb, cols = covariance.shape
    rows = row_blocks * nb
    local = covariance.reshape(rows, cols)
    p = lax.axis_index("prow")
    q = lax.axis_index("pcol")
    y, z = p // 4, p % 4
    chip, core = q // 2, q % 2
    part = rows // PIECES
    is_src = q == 0
    smem = pl.BlockSpec(memory_space=pltpu.SMEM)
    vmem = pl.BlockSpec(memory_space=pltpu.VMEM)
    hbm = pl.BlockSpec(memory_space=pl.ANY)

    messages = {}
    for chips in ((3, 7, 2, 4, 5, 1, 6, 0),):
        got = pl.pallas_call(
            functools.partial(pack_kernel, chips),
            out_shape=[jax.ShapeDtypeStruct((part + W2, W2), F32)] * len(chips),
            in_specs=[smem, hbm],
            out_specs=[hbm] * len(chips),
            scratch_shapes=[
                pltpu.VMEM((len(chips), part + W2, W2), F32),
                pltpu.SemaphoreType.DMA((len(chips), 3)),
                pltpu.SemaphoreType.DMA((len(chips),)),
            ],
            name="pack",
        )(q.reshape(1).astype(jnp.int32), local)
        messages.update(zip(chips, got))
    relay = over_pcol(messages[3], [(0, 5)]) + over_pcol(messages[7], [(0, 13)])
    mine = jnp.where(is_src, messages[0], 0.0)
    for g in (2, 4, 5, 1, 6):
        mine = mine + over_pcol(messages[g], [(0, 2 * g)])
    mine = mine + over_pcol(relay, [(5, 6), (13, 14)])
    lend = [(2 * g, 2 * g + 1) for g in range(PIECES)]
    mine = mine + over_pcol(mine, lend)
    both = mine[:part]
    pack = mine[part:].reshape(2, NB, W2)

    root = q % 4
    got = over_prow(pack, [(s, s ^ 3) for s in range(NP)])
    high = z >= 2
    pack = jnp.stack(
        [
            jnp.where(high, got[0], pack[0]),
            jnp.where(high, got[1], pack[1]),
            jnp.where(high, pack[1], got[1]),
        ]
    )
    swap = [(s, s ^ 1) for s in range(NQ)]

    def send(value, m0, m1):
        pairs = [(2 * g, 2 * chip_move(g, *m0)) for g in range(PIECES)]
        if m1 is not None:
            pairs += [(2 * g + 1, 2 * chip_move(g, *m1) + 1) for g in range(PIECES)]
        return over_pcol(value, pairs)

    def owner(m0, m1):
        own = [((chip // 2 - m[0]) % 4) * 2 + (chip + m[1]) % 2 for m in (m0, m1)]
        return [jnp.where(core == 0, own[0], own[1]), jnp.where(core == 0, own[1], own[0])]

    side = send(both, (1, 0), (-1, 0))
    later = both
    cross = send(later, (1, 1), (-1, 1))
    over = send(later, (0, 1), None)
    got = over_prow(pack, [(s, s ^ 4) for s in range(NP)])
    is_corner = jnp.arange(3)[:, None, None] == 0
    pack = jnp.where(jnp.where(is_corner, y == 1, y == root ^ 1), got, pack)
    got = over_prow(pack, [(s, s ^ 12) for s in range(NP)])
    pack = jnp.where(jnp.where(is_corner, y >= 2, y // 2 != root // 2), got, pack)
    sides = lax.optimization_barrier((pack, side, cross, over))
    got = over_prow(sides[0], [(s, s ^ 1) for s in range(NP)])
    again = send(jnp.where(core == 0, side, cross), (1, 0), (-1, 0))
    lent = over_pcol(sides[3], lend)
    side_s, cross_s, again_s = (over_pcol(value, swap) for value in (sides[1], sides[2], again))
    outer = (z == 0) | (z == 3)
    first, second = jnp.where(outer, pack, got), jnp.where(outer, got, pack)
    corner = jnp.concatenate([first[0], second[0]])
    lead = jnp.concatenate([first[1], second[1], second[2], first[2]])

    bufs = [both, over, lent, side, side_s, cross, cross_s, again, again_s]
    owners = [chip, chip // 2 * 2 + 1 - chip % 2]
    for moves in (((1, 0), (-1, 0)), ((1, 1), (-1, 1)), ((2, 0), (-2, 1))):
        owners += owner(*moves)

    info = jnp.stack([o.astype(jnp.int32) for o in owners + [core, p, q]])
    out = pl.pallas_call(
        finish_kernel,
        out_shape=jax.ShapeDtypeStruct((rows, cols), F32),
        in_specs=[smem, vmem, vmem] + [hbm] * 10,
        out_specs=hbm,
        scratch_shapes=[
            pltpu.VMEM((PIECES, part, W2), F32),
            pltpu.VMEM((PIECES, part, cols), F32),
            pltpu.VMEM((PIECES, part, cols), F32),
            pltpu.VMEM((3 * W2, cols), BF16),
            pltpu.VMEM((W2, W2), F32),
            pltpu.SemaphoreType.DMA((PIECES,)),
            pltpu.SemaphoreType.DMA((PIECES,)),
            pltpu.SemaphoreType.DMA((PIECES,)),
        ],
        compiler_params=pltpu.CompilerParams(vmem_limit_bytes=52 * 1024 * 1024),
        name="finish",
    )(info, corner, lead, *bufs, local)
    return out.reshape(row_blocks, single, nb, cols)


def solution(mesh):
    spec = P(None, "prow", None, "pcol")
    return jax.shard_map(body, mesh=mesh, in_specs=(spec,), out_specs=spec, check_vma=False)
```

```python
import functools

import jax
import jax.numpy as jnp
from jax import lax
from jax.experimental import pallas as pl
from jax.experimental.pallas import tpu as pltpu
from jax.sharding import PartitionSpec as P

AXES = ("prow", "pcol")
NP, NQ = 16, 16
NB = 64
W2 = 2 * NB
PIECES = 8
F32 = jnp.float32
BF16 = jnp.bfloat16
HI = lax.Precision.HIGHEST


def chip_move(chip, dx, dz):
    x, z = chip // 2, chip % 2
    return ((x + dx) % 4) * 2 + (z + dz) % 2


def over_pcol(value, pairs):
    flat = [(p * NQ + s, p * NQ + d) for p in range(NP) for s, d in pairs]
    return lax.ppermute(value, AXES, flat)


def over_prow(value, pairs):
    flat = [(s * NQ + q, d * NQ + q) for q in range(NQ) for s, d in pairs]
    return lax.ppermute(value, AXES, flat)


def factor(raw):
    r = lax.broadcasted_iota(jnp.int32, (W2, W2), 0)
    c = lax.broadcasted_iota(jnp.int32, (W2, W2), 1)
    low = jnp.where(r >= c, raw, 0.0)
    sym = jnp.where(r >= c, low, low.T)
    eye = jnp.where(r == c, 1.0, 0.0).astype(F32)
    nt = W2 // 8
    left = [sym[8 * t : 8 * t + 8] for t in range(nt)]
    right = [eye[8 * t : 8 * t + 8] for t in range(nt)]
    sub = lax.broadcasted_iota(jnp.int32, (8, W2), 0)
    up, inv_rows = [], []
    for k in range(nt):
        cols = {}
        for t in range(k, nt):
            for j in range(8):
                a = left[t][:, 8 * k + j : 8 * k + j + 1]
                cols[t, j] = jnp.broadcast_to(a, (8, W2))
        for s in range(0, 8, 2):
            d0 = cols[k, s][s : s + 1]
            e = cols[k, s][s + 1 : s + 2]
            d1 = cols[k, s + 1][s + 1 : s + 2]
            det = d0 * d1 - e * e
            inv0 = lax.rsqrt(d0)
            inv1 = lax.rsqrt(det) * (d0 * inv0)
            lo0, ro0 = left[k][s : s + 1] * inv0, right[k][s : s + 1] * inv0
            f10 = e * inv0
            lo1 = (left[k][s + 1 : s + 2] - f10 * lo0) * inv1
            ro1 = (right[k][s + 1 : s + 2] - f10 * ro0) * inv1
            up += [lo0, lo1]
            inv_rows += [ro0, ro1]
            piv = {}
            for j in range(s + 2, 8):
                p0 = cols[k, j][s : s + 1] * inv0
                piv[j] = (p0, (cols[k, j][s + 1 : s + 2] - f10 * p0) * inv1)
            for t in range(k, nt):
                f0 = cols[t, s] * inv0
                f1 = (cols[t, s + 1] - f0 * f10) * inv1
                if t == k:
                    f0 = jnp.where(sub > s + 1, f0, 0.0)
                    f1 = jnp.where(sub > s + 1, f1, 0.0)
                for j in range(s + 2, 8):
                    cols[t, j] = cols[t, j] - f0 * piv[j][0] - f1 * piv[j][1]
                left[t] = left[t] - f0 * lo0 - f1 * lo1
                right[t] = right[t] - f0 * ro0 - f1 * ro1
    upper = jnp.where(r <= c, jnp.concatenate(up, axis=0), 0.0)
    linv = jnp.where(r >= c, jnp.concatenate(inv_rows, axis=0), 0.0)
    return upper.T, linv, eye


def pack_kernel(chips, q_ref, local, *refs):
    outs, (held, in_sem, out_sem) = refs[:-3], refs[-3:]
    part = outs[0].shape[0] - W2

    @pl.when(q_ref[0] == 0)
    def _():
        ins, copies = [], []
        for k, g in enumerate(chips):
            ins.append([])
            for j, (src, dst, n) in enumerate(
                ((g * part, 0, part), (0, part, NB), (g // 2 * NB, part + NB, NB))
            ):
                ins[k].append(
                    pltpu.make_async_copy(
                        local.at[pl.ds(src, n), pl.ds(0, W2)],
                        held.at[k, pl.ds(dst, n)],
                        in_sem.at[k, j],
                    )
                )
                ins[k][j].start()
        for k in range(len(chips)):
            for copy in ins[k]:
                copy.wait()
            copies.append(pltpu.make_async_copy(held.at[k], outs[k], out_sem.at[k]))
            copies[k].start()
        for copy in copies:
            copy.wait()


def finish_kernel(
    info, corner_ref, lead_ref, *refs
):
    bufs, state, out = refs[:9], refs[9], refs[10]
    x_v, s_v, o_v, w_v, low_v, x_sem, s_sem, o_sem = refs[11:]
    rows, cols = s_v.shape[1:]
    core, p, q = info[8], info[9], info[10]

    def place(k):
        return pl.ds(pl.multiple_of(info[k] * rows, rows), rows)

    def load_s(k):
        return pltpu.make_async_copy(state.at[place(k)], s_v.at[k], s_sem.at[k])

    def load_x(k, ref):
        return pltpu.make_async_copy(ref, x_v.at[k], x_sem.at[k])

    def store(k):
        return pltpu.make_async_copy(o_v.at[k], out.at[place(k)], o_sem.at[k])

    for k in range(PIECES):
        load_s(k).start()
    load_x(0, bufs[0]).start()

    @pl.when(core == 0)
    def _():
        load_x(1, bufs[1]).start()

    @pl.when(core == 1)
    def _():
        load_x(1, bufs[2]).start()

    for k in range(2, PIECES):
        load_x(k, bufs[k + 1]).start()

    low, linv, eye = factor(corner_ref[...])
    low_v[...] = low
    y = lax.dot_general(
        linv, lead_ref[...], (((1,), (1,)), ((), ())), precision=HI, preferred_element_type=F32
    )
    y = jnp.concatenate([jnp.where(q == 0, -eye, y[:, :W2]), y[:, W2:]], axis=1)
    m = lax.dot_general(
        linv, y, (((0,), (0,)), ((), ())), precision=HI, preferred_element_type=F32
    )
    hi = m.astype(BF16)
    w_v[0:W2] = hi
    w_v[W2 : 2 * W2] = hi
    w_v[2 * W2 :] = (m - hi.astype(F32)).astype(BF16)

    def piece(k, carry):
        load_s(k).wait()
        load_x(k, bufs[0]).wait()
        x = x_v[k]
        xh = x.astype(BF16)
        xl = (x - xh.astype(F32)).astype(BF16)
        prod = jnp.dot(jnp.concatenate([xh, xl, xh], axis=1), w_v[...], preferred_element_type=F32)
        lane = lax.broadcasted_iota(jnp.int32, (1, cols), 1)
        replaced = (q == 0) & (lane < W2)
        o_v[k] = jnp.where(replaced, 0.0, s_v[k]) - prod

        @pl.when(info[k] == 0)
        def _():
            top = 4 * NB
            rr = lax.broadcasted_iota(jnp.int32, (top, cols), 0)
            cc = lax.broadcasted_iota(jnp.int32, (top, cols), 1) + q * cols
            rg = ((rr // NB) * NP + p) * NB + rr % NB
            o_v[k, 0:top] = jnp.where(rg >= cc, o_v[k, 0:top], s_v[k, 0:top])

        @pl.when((info[k] == 0) & (q == 0) & (p < 2))
        def _():
            rr = lax.broadcasted_iota(jnp.int32, (NB, W2), 0) + p * NB
            cc = lax.broadcasted_iota(jnp.int32, (NB, W2), 1)
            part = low_v[pl.ds(pl.multiple_of(jnp.minimum(p, 1) * NB, NB), NB), :]
            o_v[k, 0:NB, 0:W2] = jnp.where(rr >= cc, part, s_v[k, 0:NB, 0:W2])

        store(k).start()
        return carry

    lax.fori_loop(0, PIECES, piece, 0)
    for k in range(PIECES):
        store(k).wait()


def body(covariance):
    row_blocks, single, nb, cols = covariance.shape
    rows = row_blocks * nb
    local = covariance.reshape(rows, cols)
    p = lax.axis_index("prow")
    q = lax.axis_index("pcol")
    y, z = p // 4, p % 4
    chip, core = q // 2, q % 2
    part = rows // PIECES
    is_src = q == 0
    smem = pl.BlockSpec(memory_space=pltpu.SMEM)
    vmem = pl.BlockSpec(memory_space=pltpu.VMEM)
    hbm = pl.BlockSpec(memory_space=pl.ANY)

    messages = {}
    for chips in ((3, 7, 5, 2, 4, 1, 6, 0),):
        got = pl.pallas_call(
            functools.partial(pack_kernel, chips),
            out_shape=[jax.ShapeDtypeStruct((part + W2, W2), F32)] * len(chips),
            in_specs=[smem, hbm],
            out_specs=[hbm] * len(chips),
            scratch_shapes=[
                pltpu.VMEM((len(chips), part + W2, W2), F32),
                pltpu.SemaphoreType.DMA((len(chips), 3)),
                pltpu.SemaphoreType.DMA((len(chips),)),
            ],
            name="pack",
        )(q.reshape(1).astype(jnp.int32), local)
        messages.update(zip(chips, got))
    relay = over_pcol(messages[3], [(0, 5)]) + over_pcol(messages[7], [(0, 13)])
    mine = jnp.where(is_src, messages[0], 0.0)
    for g in (5, 2, 4, 1, 6):
        mine = mine + over_pcol(messages[g], [(0, 2 * g)])
    mine = mine + over_pcol(relay, [(5, 6), (13, 14)])
    lend = [(2 * g, 2 * g + 1) for g in range(PIECES)]
    mine = mine + over_pcol(mine, lend)
    both = mine[:part]
    pack = mine[part:].reshape(2, NB, W2)

    root = q % 4
    got = over_prow(pack, [(s, s ^ 3) for s in range(NP)])
    high = z >= 2
    pack = jnp.stack(
        [
            jnp.where(high, got[0], pack[0]),
            jnp.where(high, got[1], pack[1]),
            jnp.where(high, pack[1], got[1]),
        ]
    )
    swap = [(s, s ^ 1) for s in range(NQ)]

    def send(value, m0, m1):
        pairs = [(2 * g, 2 * chip_move(g, *m0)) for g in range(PIECES)]
        if m1 is not None:
            pairs += [(2 * g + 1, 2 * chip_move(g, *m1) + 1) for g in range(PIECES)]
        return over_pcol(value, pairs)

    def owner(m0, m1):
        own = [((chip // 2 - m[0]) % 4) * 2 + (chip + m[1]) % 2 for m in (m0, m1)]
        return [jnp.where(core == 0, own[0], own[1]), jnp.where(core == 0, own[1], own[0])]

    side = send(both, (1, 0), (-1, 0))
    later = both
    cross = send(later, (1, 1), (-1, 1))
    over = send(later, (0, 1), None)
    got = over_prow(pack, [(s, s ^ 4) for s in range(NP)])
    is_corner = jnp.arange(3)[:, None, None] == 0
    pack = jnp.where(jnp.where(is_corner, y == 1, y == root ^ 1), got, pack)
    got = over_prow(pack, [(s, s ^ 12) for s in range(NP)])
    pack = jnp.where(jnp.where(is_corner, y >= 2, y // 2 != root // 2), got, pack)
    sides = lax.optimization_barrier((pack, side, cross, over))
    got = over_prow(sides[0], [(s, s ^ 1) for s in range(NP)])
    again = send(jnp.where(core == 0, side, cross), (1, 0), (-1, 0))
    lent = over_pcol(sides[3], lend)
    side_s, cross_s, again_s = (over_pcol(value, swap) for value in (sides[1], sides[2], again))
    outer = (z == 0) | (z == 3)
    first, second = jnp.where(outer, pack, got), jnp.where(outer, got, pack)
    corner = jnp.concatenate([first[0], second[0]])
    lead = jnp.concatenate([first[1], second[1], second[2], first[2]])

    bufs = [both, over, lent, side, side_s, cross, cross_s, again, again_s]
    owners = [chip, chip // 2 * 2 + 1 - chip % 2]
    for moves in (((1, 0), (-1, 0)), ((1, 1), (-1, 1)), ((2, 0), (-2, 1))):
        owners += owner(*moves)

    info = jnp.stack([o.astype(jnp.int32) for o in owners + [core, p, q]])
    out = pl.pallas_call(
        finish_kernel,
        out_shape=jax.ShapeDtypeStruct((rows, cols), F32),
        in_specs=[smem, vmem, vmem] + [hbm] * 10,
        out_specs=hbm,
        scratch_shapes=[
            pltpu.VMEM((PIECES, part, W2), F32),
            pltpu.VMEM((PIECES, part, cols), F32),
            pltpu.VMEM((PIECES, part, cols), F32),
            pltpu.VMEM((3 * W2, cols), BF16),
            pltpu.VMEM((W2, W2), F32),
            pltpu.SemaphoreType.DMA((PIECES,)),
            pltpu.SemaphoreType.DMA((PIECES,)),
            pltpu.SemaphoreType.DMA((PIECES,)),
        ],
        compiler_params=pltpu.CompilerParams(vmem_limit_bytes=52 * 1024 * 1024),
        name="finish",
    )(info, corner, lead, *bufs, local)
    return out.reshape(row_blocks, single, nb, cols)


def solution(mesh):
    spec = P(None, "prow", None, "pcol")
    return jax.shard_map(body, mesh=mesh, in_specs=(spec,), out_specs=spec, check_vma=False)
```
